128 devices in a mesh: grp: 2 (over y_lo), row: 8 (over x, core), col: 8 (over z, y_hi).
Axes of the slice: x: 4, y: 4 (y_hi: 2, y_lo: 2; y = y_hi * 2 + y_lo), z: 4, core: 2. Of those that a mesh axis runs over, the one named last changes fastest.
Arguments:
- root_inverse: float32 [4096, 4096], P('row', ('grp', 'col')), as said below
- ancestor_map: int32 [2, 2048], P('grp'), may hold values from 0 to 4095, as said below
- live_rows: int32 [2], P('grp'), may hold values from 512 to 2048, as said below
- factor_below: float32 [2, 2048, 3072], P('grp', 'row', 'col'), may hold values from -0.125 to 0.125
- diag_inverse: float32 [2, 3072, 3072], P('grp', 'row', 'col'), as said below
- tile_mask: int32 [2, 16, 24], P('grp', 'row', 'col'), may hold values 0 or 1
Outputs:
- below_inverse: float32 [2, 2048, 3072], P('grp', 'row', 'col')
- separator_inverse: float32 [2, 3072, 3072], P('grp', 'row', 'col')
The draws below stay inside these ranges and needn't reach their ends.
Inputs may be any that keep to these rules, and one draw needn't show every extreme that they name: `ancestor_map`: within each front the map's 2048 entries are distinct root rows in an order drawn from the seed; 0 and 4095 are among them. `live_rows`: front 0 uses all 2048 rows. `root_inverse`: symmetric with a positive diagonal. `diag_inverse`: lower triangular with a positive diagonal.
All inputs are finite; a program needn't handle non-finite values. No bound on the sum of `tile_mask` on one device may be relied on, other than what follows from the above.
Results may differ from the reference program's by a relative error of at most 0.0001.
Values sent between devices are 32-bit elements; how exact they have to be, the bound alone decides.
No kernel may reach another device: no remote copies, remote signals or barrier semaphores. Data moves between devices by JAX's collectives and lax.ppermute only.
A program may use at most 128 MiB of HBM per device.

```python
import math
import jax
import jax.numpy as jnp
from jax import lax

ROOT = 4096
SEP = 3072
ANC = 2048
TILE = 128
CHILDREN = 2


def draw_root_inverse(key, part):
    key = jax.random.fold_in(key, 11)
    first_key, second_key = jax.random.split(key, 2)
    entries = jax.random.normal(first_key, (ROOT, ROOT), jnp.float32)
    symmetric = (entries + entries.T) * (0.35 / math.sqrt(ROOT))
    rows_at = jnp.arange(ROOT)[:, None]
    cols_at = jnp.arange(ROOT)[None, :]
    diagonal = jnp.exp(jax.random.uniform(second_key, (ROOT,), jnp.float32, math.log(2.0), math.log(4.0)))
    matrix = jnp.where(rows_at == cols_at, diagonal[:, None], symmetric)
    return matrix.astype(jnp.float32)


def draw_diag_inverse(key, part):
    key = jax.random.fold_in(key, 23)
    first_key, second_key = jax.random.split(key)
    entries = jax.random.normal(first_key, (2, SEP, SEP), jnp.float32)
    diagonal = jax.random.uniform(second_key, (2, SEP, 1), jnp.float32, 1.0, 2.0)
    rows_at = jnp.arange(SEP)[:, None]
    cols_at = jnp.arange(SEP)[None, :]
    lower = jnp.where(rows_at > cols_at, entries * (0.7 / math.sqrt(SEP)), 0.0)
    matrix = jnp.where(rows_at == cols_at, diagonal, lower)
    return matrix.astype(jnp.float32)


def draw_ancestor_map(key, part):
    key = jax.random.fold_in(key, 37)
    fronts = []
    for child in range(2):
        child_key = jax.random.fold_in(key, child)
        pick_key, order_key = jax.random.split(child_key)
        chosen = jax.random.permutation(pick_key, ROOT - 2)[:ANC - 2] + 1
        joined = jnp.concatenate([jnp.zeros((1,), jnp.int32), chosen.astype(jnp.int32), jnp.full((1,), ROOT - 1, jnp.int32)])
        order = jax.random.permutation(order_key, ANC)
        fronts.append(joined[order])
    return jnp.stack(fronts).astype(jnp.int32)


def draw_live_rows(key, part):
    key = jax.random.fold_in(key, 41)
    other = jax.random.randint(key, (1,), ANC // 4, ANC)
    return jnp.concatenate([jnp.full((1,), ANC, jnp.int32), other.astype(jnp.int32)])


def with_ends(array, own_key, smallest, top_value):
    place = [jax.random.randint(jax.random.fold_in(own_key, axis), (), 0, length) for axis, length in enumerate(array.shape)]
    longest = array.shape.index(max(array.shape))
    beside = place[:longest] + [(place[longest] + 1) % array.shape[longest]] + place[longest + 1:]
    return array.at[tuple(place)].set(smallest).at[tuple(beside)].set(top_value)


def block_scale(stream_key, shape, cuts, smallest, top_value):
    def one(axis_at, blocks):
        draws = jax.random.uniform(jax.random.fold_in(jax.random.fold_in(stream_key, 6), axis_at), (blocks,), jnp.float32, smallest / len(cuts), top_value / len(cuts))
        return jnp.repeat(jnp.exp(draws), shape[axis_at] // blocks).reshape((-1,) + (1,) * (len(shape) - axis_at - 1))

    loudness = one(*cuts[0])
    for cut in cuts[1:]:
        loudness = loudness * one(*cut)
    return loudness


def gaussian(key, extent, width, reach, cuts=(), kind=jnp.bfloat16):
    values = width * jax.random.normal(key, extent, jnp.float32)
    if cuts:
        values = values * block_scale(key, extent, cuts, -0.22, 0.18)
    return jnp.clip(values, -reach, reach).astype(kind)


def setup_inputs(seed: int = 0) -> dict:
    splits = jax.random.split(jax.random.key(seed), 7)
    root_inverse = draw_root_inverse(jax.random.fold_in(splits[6], 71), 0)
    ancestor_map = draw_ancestor_map(jax.random.fold_in(splits[6], 71), 0)
    live_rows = draw_live_rows(jax.random.fold_in(splits[6], 71), 0)
    factor_below = gaussian(splits[3], (CHILDREN, ANC, SEP), ANC ** -0.5, 0.125, ((0, 2), (1, 8), (2, 8)), jnp.float32)
    diag_inverse = draw_diag_inverse(jax.random.fold_in(splits[6], 71), 0)
    tile_mask = with_ends((jax.random.randint(splits[5], (CHILDREN, ANC // TILE, SEP // TILE), 0, 2) < 1).astype(jnp.int32), jax.random.fold_in(splits[5], 1), 0, 1)
    return dict(root_inverse=root_inverse, ancestor_map=ancestor_map, live_rows=live_rows, factor_below=factor_below, diag_inverse=diag_inverse, tile_mask=tile_mask)


highest = lax.Precision.HIGHEST


def one_front(root_inverse, ancestor_ids, live_count, below, diag_block, tile_keep):
    keep = jnp.repeat(jnp.repeat(tile_keep, TILE, axis=0), TILE, axis=1).astype(jnp.float32)
    retained = below * keep
    update = jnp.dot(retained, diag_block, precision=highest, preferred_element_type=jnp.float32)
    live_flag = jnp.arange(ANC, dtype=jnp.int32) < live_count
    update = jnp.where(live_flag[:, None], update, jnp.float32(0.0))
    spread = jnp.zeros((ROOT, SEP), jnp.float32).at[ancestor_ids].add(update)
    product = jnp.dot(root_inverse, spread, precision=highest, preferred_element_type=jnp.float32)
    coupling = jnp.where(live_flag[:, None], -product[ancestor_ids], jnp.float32(0.0))
    gram = jnp.dot(diag_block.T, diag_block, precision=highest, preferred_element_type=jnp.float32)
    cross = jnp.dot(update.T, coupling, precision=highest, preferred_element_type=jnp.float32)
    return coupling, gram - cross


def reference(root_inverse, ancestor_map, live_rows, factor_below, diag_inverse, tile_mask):
    below_parts = []
    separator_parts = []
    for child in range(2):
        coupling, separator = one_front(root_inverse, ancestor_map[child], live_rows[child],
                                        factor_below[child], diag_inverse[child], tile_mask[child])
        below_parts.append(coupling)
        separator_parts.append(separator)
    return jnp.stack(below_parts), jnp.stack(separator_parts)
```

```python
import functools

import jax
import jax.numpy as jnp
from jax import lax
from jax.experimental import pallas as pl
from jax.experimental.pallas import tpu as pltpu
from jax.sharding import PartitionSpec as P

ROOT = 4096
SEP = 3072
ANC = 2048
TILE = 128
ROWS = 8
COLS = 8
BAND = ANC // ROWS
WIDE = SEP // COLS
KEEP = ROOT // (2 * COLS)

f32 = jnp.float32
bf16 = jnp.bfloat16
VMEM = pl.BlockSpec(memory_space=pltpu.VMEM)
SMEM = pl.BlockSpec(memory_space=pltpu.SMEM)


def shift_z(x, step):
    pairs = [(c, (c // 2 + step) % 4 * 2 + c % 2) for c in range(COLS)]
    return lax.ppermute(x, "col", pairs)


def swap_y(x):
    return lax.ppermute(x, "col", [(c, c ^ 1) for c in range(COLS)])


def swap_group(x):
    return lax.ppermute(x, "grp", [(0, 1), (1, 0)])


COL_ORDER = ((0, 0), (-1, 0), (1, 0), (2, 0), (0, 1), (-1, 1), (1, 1), (2, 1))


def gather_col(x):
    n = x.shape[0] // 2
    before = shift_z(x, 1)
    after = shift_z(x, -1)
    other = swap_y(x)
    far_top = shift_z(before[:n], 1)
    far_low = shift_z(after[n:], -1)
    other_before_low = swap_y(before[n:])
    other_after_top = swap_y(after[:n])
    other_before_top = shift_z(other[:n], 1)
    other_after_low = shift_z(other[n:], -1)
    other_far_top = shift_z(other_before_top, 1)
    other_far_low = shift_z(other_after_low, -1)
    return [
        x[:n], x[n:],
        before[:n], before[n:],
        after[:n], after[n:],
        far_top, far_low,
        other[:n], other[n:],
        other_before_top, other_before_low,
        other_after_top, other_after_low,
        other_far_top, other_far_low,
    ]


def col_ids():
    c = lax.axis_index("col")
    z, y = c // 2, c % 2
    return jnp.stack([(z + dz) % 4 * 2 + jnp.bitwise_xor(y, dy) for dz, dy in COL_ORDER]).astype(jnp.int32)


def split(x):
    high = x.astype(bf16)
    return high, (x - high.astype(f32)).astype(bf16)


def dot(a, b):
    return jnp.dot(a, b, preferred_element_type=f32)


def dot3(a, b):
    return dot(a[0], b[0]) + (dot(a[0], b[1]) + dot(a[1], b[0]))


def params(mib):
    return pltpu.CompilerParams(vmem_limit_bytes=mib * 2**20)


def update_kernel(ids, live, diag, *rest):
    halves, (update_ref, flipped_ref) = rest[:16], rest[16:]
    total = jnp.zeros((BAND, WIDE), f32)
    for p in range(8):
        block = split(diag[pl.ds(pl.multiple_of(ids[p] * WIDE, WIDE), WIDE), :])
        piece = split(jnp.concatenate([halves[2 * p][...], halves[2 * p + 1][...]], axis=0))
        total += dot3(piece, block)
    row = ids[8] + lax.broadcasted_iota(jnp.int32, (BAND, WIDE), 0)
    total = jnp.where(row < live[0], total, 0.0)
    update_ref[...] = total
    flipped_ref[...] = total.T


def pick_kernel(place, *rest):
    halves, (high_ref, low_ref) = rest[:16], rest[16:18]
    source_high, source_low = rest[18:]
    for p in range(16):
        high, low = split(halves[p][...])
        at = p * KEEP
        source_high[:, at:at + KEEP] = high
        source_low[:, at:at + KEEP] = low

    step = 256

    def body(j, carry):
        at = pl.ds(pl.multiple_of(j * step, step), step)
        where = place[:, at]
        hot = jnp.where(lax.broadcasted_iota(jnp.int32, (ROOT, step), 0) == where, 1.0, 0.0).astype(bf16)
        high_ref[:, at] = dot(source_high[...], hot).astype(bf16)
        low_ref[:, at] = dot(source_low[...], hot).astype(bf16)
        return carry

    lax.fori_loop(0, ANC // step, body, 0)


def coupling_kernel(ids, live, high, low, update, out_ref):
    total = jnp.zeros((BAND, WIDE), f32)
    for p in range(4):
        at = slice(p * 512, p * 512 + 512)
        total += dot3((high[:, at], low[:, at]), split(update[at, :]))
    row = ids[8] + lax.broadcasted_iota(jnp.int32, (BAND, WIDE), 0)
    out_ref[...] = jnp.where(row < live[0], -total, 0.0)


def separator_kernel(ids, diag, coupling, *rest):
    diag_halves, update_halves, out_ref = rest[:16], rest[16:32], rest[32]
    n = WIDE // 2
    right_diag, right_coupling = split(diag[...]), split(-coupling[...])
    for p in range(8):
        left = split(jnp.concatenate([diag_halves[2 * p][...], diag_halves[2 * p + 1][...]], axis=0))
        total = dot3(left, right_diag)
        left = split(jnp.concatenate([update_halves[2 * p][...], update_halves[2 * p + 1][...]], axis=0))
        total += dot3(left, right_coupling)
        out_ref[pl.ds(pl.multiple_of(ids[p] * WIDE, WIDE), WIDE), :] = total


def per_device(root_inverse, ancestor_map, live_rows, factor_below, diag_inverse, tile_mask):
    row = lax.axis_index("row")
    group = lax.axis_index("grp")
    first_row = row * BAND
    ids = jnp.concatenate([col_ids(), first_row[None].astype(jnp.int32)])
    diag_block = diag_inverse[0]

    root_cols = lax.all_gather(root_inverse, "row", axis=0, tiled=True)
    diag_cols = lax.all_gather(diag_block, "row", axis=0, tiled=True)

    tile_keep = jnp.repeat(jnp.repeat(tile_mask[0], TILE, axis=0), TILE, axis=1).astype(f32)
    retained = factor_below[0] * tile_keep
    retained_all = gather_col(retained)

    update, update_flipped = pl.pallas_call(
        update_kernel,
        out_shape=(jax.ShapeDtypeStruct((BAND, WIDE), f32), jax.ShapeDtypeStruct((WIDE, BAND), f32)),
        in_specs=[SMEM, SMEM] + [VMEM] * 17,
        out_specs=(VMEM, VMEM),
        compiler_params=params(40),
    )(ids, live_rows, diag_cols, *retained_all)

    own_map = ancestor_map[0]
    other_map = swap_group(own_map)
    own_rows = root_cols[lax.dynamic_slice_in_dim(own_map, first_row, BAND)]
    other_rows = swap_group(root_cols[lax.dynamic_slice_in_dim(other_map, first_row, BAND)])
    picked = gather_col(jnp.concatenate([own_rows, other_rows], axis=0))
    rel = jnp.zeros((COLS,), jnp.int32).at[col_ids()].set(jnp.arange(COLS, dtype=jnp.int32))
    half = (own_map // (ROOT // 2) != group).astype(jnp.int32)
    place = rel[own_map % (ROOT // 2) // KEEP] * (2 * KEEP) + half * KEEP + own_map % KEEP
    high, low = pl.pallas_call(
        pick_kernel,
        out_shape=(jax.ShapeDtypeStruct((BAND, ANC), bf16), jax.ShapeDtypeStruct((BAND, ANC), bf16)),
        in_specs=[VMEM] * 17,
        out_specs=(VMEM, VMEM),
        scratch_shapes=[pltpu.VMEM((BAND, ROOT), bf16), pltpu.VMEM((BAND, ROOT), bf16)],
        compiler_params=params(40),
    )(place[None, :], *picked)

    update_cols = lax.all_gather(update, "row", axis=0, tiled=True)
    coupling = pl.pallas_call(
        coupling_kernel,
        out_shape=jax.ShapeDtypeStruct((BAND, WIDE), f32),
        in_specs=[SMEM, SMEM] + [VMEM] * 3,
        out_specs=VMEM,
        compiler_params=params(40),
    )(ids, live_rows, high, low, update_cols)

    update_all = gather_col(update_flipped)
    diag_all = gather_col(diag_block.T)
    partial = pl.pallas_call(
        separator_kernel,
        out_shape=jax.ShapeDtypeStruct((SEP, WIDE), f32),
        in_specs=[SMEM] + [VMEM] * 34,
        out_specs=VMEM,
        compiler_params=params(48),
    )(ids, diag_block, coupling, *diag_all, *update_all)
    separator = lax.psum_scatter(partial, "row", scatter_dimension=0, tiled=True)
    return (coupling[None], separator[None])


def solution(mesh):
    return jax.shard_map(
        per_device,
        mesh=mesh,
        in_specs=(
            P("row", ("grp", "col")),
            P("grp", None),
            P("grp"),
            P("grp", "row", "col"),
            P("grp", "row", "col"),
            P("grp", "row", "col"),
        ),
        out_specs=(P("grp", "row", "col"), P("grp", "row", "col")),
        check_vma=False,
    )
```

```python
import functools

import jax
import jax.numpy as jnp
from jax import lax
from jax.experimental import pallas as pl
from jax.experimental.pallas import tpu as pltpu
from jax.sharding import PartitionSpec as P

ROOT = 4096
SEP = 3072
ANC = 2048
TILE = 128
SIDE = 8
BAND = ANC // SIDE
WIDE = SEP // SIDE
KEEP = ROOT // (2 * SIDE)

f32 = jnp.float32
bf16 = jnp.bfloat16
VMEM = pl.BlockSpec(memory_space=pltpu.VMEM)
SMEM = pl.BlockSpec(memory_space=pltpu.SMEM)
ANY = pl.BlockSpec(memory_space=pl.ANY)


def hold(arrays, deps):
    n = len(arrays)
    return pl.pallas_call(
        lambda *refs: None,
        out_shape=[jax.ShapeDtypeStruct(x.shape, x.dtype) for x in arrays],
        in_specs=[ANY] * (n + len(deps)),
        out_specs=[ANY] * n,
        input_output_aliases={i: i for i in range(n)},
        compiler_params=pltpu.CompilerParams(vmem_limit_bytes=60 * 2**20),
    )(*arrays, *deps)


def shift(x, axis, step):
    return lax.ppermute(x, axis, [(i, (i // 2 + step) % 4 * 2 + i % 2) for i in range(SIDE)])


def swap(x, axis):
    return lax.ppermute(x, axis, [(i, i ^ 1) for i in range(SIDE)])


def swap_group(x):
    return lax.ppermute(x, "grp", [(0, 1), (1, 0)])


ORDER = ((0, 0), (-1, 0), (1, 0), (2, 0), (0, 1), (-1, 1), (1, 1), (2, 1))


def near_col(x):
    return [x, shift(x, "col", 1), shift(x, "col", -1), shift(x, "col", 2), swap(x, "col")]


def rest_col(far, other):
    return [shift(other, "col", 1), shift(other, "col", -1), swap(far, "col")]


def gather_col(x, meanwhile=()):
    *near, far, other = near_col(x)
    far, other, *rest = hold([far, other, *meanwhile], near[1:])
    return [*near, far, other, *rest_col(far, other)], rest


def fetch(refs, buffer, sems):
    copies = [pltpu.make_async_copy(ref, buffer.at[p], sems.at[p]) for p, ref in enumerate(refs)]
    for copy in copies:
        copy.start()
    return copies


def ids_of(axis):
    i = lax.axis_index(axis)
    return jnp.stack([(i // 2 + ring) % 4 * 2 + jnp.bitwise_xor(i % 2, pair) for ring, pair in ORDER]).astype(jnp.int32)


def place_of(block, axis):
    i = lax.axis_index(axis)
    ring = (block // 2 - i // 2) % 4
    first = jnp.where(ring == 3, 1, jnp.where(ring == 0, 0, ring + 1))
    return first + 4 * jnp.bitwise_xor(block % 2, i % 2)


def split(x):
    high = x.astype(bf16)
    return high, (x - high.astype(f32)).astype(bf16)


def dot(a, b):
    return jnp.dot(a, b, preferred_element_type=f32)


def dot3(a, b):
    return dot(a[0], b[0]) + (dot(a[0], b[1]) + dot(a[1], b[0]))


def call(kernel, out, scalars, blocks, arrays, scratch, copies, work):
    return pl.pallas_call(
        kernel,
        out_shape=out,
        in_specs=[SMEM] * len(scalars) + [VMEM] * len(blocks) + [ANY] * len(arrays),
        out_specs=jax.tree.map(lambda _: VMEM, out),
        scratch_shapes=[pltpu.VMEM(s, d) for s, d in scratch] + [pltpu.SemaphoreType.DMA((copies,))],
        compiler_params=pltpu.CompilerParams(vmem_limit_bytes=60 * 2**20),
        cost_estimate=pl.CostEstimate(flops=work * 10**9, bytes_accessed=work * 3 * 10**6, transcendentals=0),
    )(*scalars, *blocks, *arrays)


def array(*shape, dtype=f32):
    return jax.ShapeDtypeStruct(shape, dtype)


def update_sum(cols, below, diag, below_buf, diag_buf, sems):
    n = len(below)
    below_in = fetch(below, below_buf, sems)
    diag_in = [
        pltpu.make_async_copy(
            diag.at[pl.ds(pl.multiple_of(cols[p] * WIDE, WIDE), WIDE)], diag_buf.at[p], sems.at[n + p]
        )
        for p in range(n)
    ]
    for copy in diag_in:
        copy.start()
    total = jnp.zeros((BAND, WIDE), f32)
    for p in range(n):
        below_in[p].wait()
        diag_in[p].wait()
        total += dot3(split(below_buf[p]), split(diag_buf[p]))
    return total


def update_near_kernel(cols, *rest):
    out, *scratch = rest[6:]
    out[...] = update_sum(cols, rest[:5], rest[5], *scratch)


def update_kernel(cols, row, live, part, *rest):
    flipped, *scratch = rest[4:]
    total = part[...] + update_sum(cols, rest[:3], rest[3], *scratch)
    ids = row[0] * BAND + lax.broadcasted_iota(jnp.int32, (BAND, WIDE), 0)
    flipped[...] = jnp.where(ids < live[0], total, 0.0).T


def pick_rows(place, source, out, first, count):
    step = 32

    def body(j, carry):
        at = pl.multiple_of(j * step, step)
        for i in range(0, step, 8):
            found = [source[pl.ds(place[first + at + i + k], 1), :] for k in range(8)]
            out[pl.ds(at + i, 8), :] = jnp.concatenate(found, axis=0)
        return carry

    lax.fori_loop(0, count // step, body, 0)


def root_rows_kernel(place, root, _, own, other, source, found, sems):
    copy = pltpu.make_async_copy(root, source, sems.at[0])
    copy.start()
    copy.wait()
    for half, out in enumerate((own, other)):
        pick_rows(place, source, found, half * BAND, BAND)
        out[...] = found[...].T


def coupling_kernel(place, row, live, *rest):
    update, pieces, out, update_buf, source, found, sems = rest[0], rest[1:9], *rest[9:]
    update_in = [
        pltpu.make_async_copy(update.at[pl.ds(p * WIDE, WIDE)], update_buf.at[p], sems.at[8 + p]) for p in range(8)
    ]
    pieces_in = [
        pltpu.make_async_copy(pieces[p], source.at[pl.ds(p * 2 * KEEP, 2 * KEEP)], sems.at[p]) for p in range(8)
    ]
    for copy in pieces_in + update_in:
        copy.start()
    for copy in pieces_in:
        copy.wait()
    total = jnp.zeros((WIDE, BAND), f32)
    for p in range(8):
        pick_rows(place, source, found, p * BAND, BAND)
        update_in[p].wait()
        total += dot3(split(update_buf[p]), split(found[...]))
    ids = row[0] * BAND + lax.broadcasted_iota(jnp.int32, (BAND, WIDE), 0)
    out[...] = jnp.where(ids < live[0], -total.T, 0.0)


def gram_kernel(diag, *rest):
    pieces, out, buffer, sems = rest[:8], *rest[9:]
    copies = fetch(pieces, buffer, sems)
    right = split(diag[...])
    for p in range(8):
        copies[p].wait()
        out[p] = dot3(split(buffer[p].T), right)


def partial_kernel(first, count, cols, coupling, *rest):
    update, gram, out, update_buf, gram_buf, out_buf, sems = rest[:count], rest[count], *rest[-5:]
    update_in = fetch(update, update_buf, sems)
    gram_in = [
        pltpu.make_async_copy(gram.at[first + p], gram_buf.at[p], sems.at[count + p]) for p in range(count)
    ]
    for copy in gram_in:
        copy.start()
    right = split(-coupling[...])
    sent = []
    for p in range(count):
        update_in[p].wait()
        gram_in[p].wait()
        out_buf[p] = gram_buf[p] + dot3(split(update_buf[p]), right)
        at = pl.ds(pl.multiple_of(cols[first + p] * WIDE, WIDE), WIDE)
        sent.append(pltpu.make_async_copy(out_buf.at[p], out.at[at], sems.at[2 * count + p]))
        sent[-1].start()
    for copy in sent:
        copy.wait()


def partial(first, update, cols, coupling, gram, onto=None):
    count = len(update)
    given = [cols, coupling, *update, gram] + ([] if onto is None else [onto])
    return pl.pallas_call(
        functools.partial(partial_kernel, first, count),
        out_shape=array(SEP, WIDE),
        in_specs=[SMEM, VMEM] + [ANY] * (len(given) - 2),
        out_specs=ANY,
        scratch_shapes=[
            pltpu.VMEM((count, WIDE, BAND), f32),
            pltpu.VMEM((count, WIDE, WIDE), f32),
            pltpu.VMEM((count, WIDE, WIDE), f32),
            pltpu.SemaphoreType.DMA((3 * count,)),
        ],
        input_output_aliases={} if onto is None else {len(given) - 1: 0},
        compiler_params=pltpu.CompilerParams(vmem_limit_bytes=60 * 2**20),
        cost_estimate=pl.CostEstimate(flops=count * 10**9, bytes_accessed=count * 3 * 10**6, transcendentals=0),
    )(*given)


def per_device(root_inverse, ancestor_map, live_rows, factor_below, diag_inverse, tile_mask):
    row, group = lax.axis_index("row"), lax.axis_index("grp")
    cols = ids_of("col")
    diag_block = diag_inverse[0]
    own_map = ancestor_map[0]
    other_map = swap_group(own_map)

    root_cols = lax.all_gather(root_inverse, "row", axis=0, tiled=True)

    diag_cols = lax.all_gather(diag_block, "row", axis=0, tiled=True)

    diag_all = near_col(diag_block)
    diag_all += rest_col(*diag_all[3:])
    tile_keep = jnp.repeat(jnp.repeat(tile_mask[0], TILE, axis=0), TILE, axis=1).astype(f32)
    below, other_map = hold([factor_below[0] * tile_keep, other_map[None]], diag_all)

    gram = call(
        gram_kernel, array(SIDE, WIDE, WIDE), [], [diag_block], diag_all + [below], [((SIDE, WIDE, WIDE), f32)], 8, 12
    )
    place = jnp.concatenate([lax.dynamic_slice_in_dim(m, row * BAND, BAND) for m in (own_map, other_map[0])])
    own_rows, other_rows = call(
        root_rows_kernel, (array(KEEP, BAND), array(KEEP, BAND)), [place], [], [root_cols, below],
        [((ROOT, KEEP), f32), ((BAND, KEEP), f32)], 1, 5,
    )
    below_near = near_col(below)
    *below_near, gram, other_rows = hold([*below_near, gram, swap_group(other_rows)], [])
    below_rest = rest_col(*below_near[3:])
    part = call(
        update_near_kernel, array(BAND, WIDE), [cols[:5]], [], below_near + [diag_cols],
        [((5, BAND, WIDE), f32), ((5, WIDE, WIDE), f32)], 10, 5,
    )
    picked = jnp.concatenate([own_rows, other_rows], axis=0)
    picked, part = hold([picked, part], below_rest)

    flipped = call(
        update_kernel, array(WIDE, BAND), [cols[5:], row[None], live_rows], [part], below_rest + [diag_cols],
        [((3, BAND, WIDE), f32), ((3, WIDE, WIDE), f32)], 6, 3,
    )
    update_rows = lax.all_gather(flipped, "row", axis=0, tiled=True)
    picked_all = near_col(picked)
    picked_all += rest_col(*picked_all[3:])
    flipped, gram = hold([flipped, gram], picked_all)

    half = (own_map // (ROOT // 2) != group).astype(jnp.int32)
    place = place_of(own_map % (ROOT // 2) // KEEP, "col") * (2 * KEEP) + half * KEEP + own_map % KEEP
    coupling = call(
        coupling_kernel, array(BAND, WIDE), [place, row[None], live_rows], [], [update_rows] + picked_all,
        [((SIDE, WIDE, BAND), f32), ((ROOT, BAND), f32), ((BAND, BAND), f32)], 16, 12,
    )
    update_near = near_col(flipped)
    update_near = hold(update_near, [coupling])
    update_rest = rest_col(*update_near[3:])
    total = partial(0, update_near, cols, coupling, gram)
    (total,) = hold([total], update_rest)
    total = partial(5, update_rest, cols, coupling, gram, total)
    separator = lax.psum_scatter(total, "row", scatter_dimension=0, tiled=True)
    return (coupling[None], separator[None])


def solution(mesh):
    return jax.shard_map(
        per_device,
        mesh=mesh,
        in_specs=(
            P("row", ("grp", "col")),
            P("grp", None),
            P("grp"),
            P("grp", "row", "col"),
            P("grp", "row", "col"),
            P("grp", "row", "col"),
        ),
        out_specs=(P("grp", "row", "col"), P("grp", "row", "col")),
        check_vma=False,
    )
```

```python
import functools

import jax
import jax.numpy as jnp
from jax import lax
from jax.experimental import pallas as pl
from jax.experimental.pallas import tpu as pltpu
from jax.sharding import PartitionSpec as P

ROOT = 4096
SEP = 3072
ANC = 2048
TILE = 128
SIDE = 8
BAND = ANC // SIDE
WIDE = SEP // SIDE
KEEP = ROOT // (2 * SIDE)

f32 = jnp.float32
bf16 = jnp.bfloat16
VMEM = pl.BlockSpec(memory_space=pltpu.VMEM)
SMEM = pl.BlockSpec(memory_space=pltpu.SMEM)
ANY = pl.BlockSpec(memory_space=pl.ANY)

def hold(arrays, deps):
    n = len(arrays)
    return pl.pallas_call(
        lambda *refs: None,
        out_shape=[jax.ShapeDtypeStruct(x.shape, x.dtype) for x in arrays],
        in_specs=[ANY] * (n + len(deps)),
        out_specs=[ANY] * n,
        input_output_aliases={i: i for i in range(n)},
        compiler_params=pltpu.CompilerParams(vmem_limit_bytes=60 * 2**20),
    )(*arrays, *deps)

def shift(x, axis, step):
    return lax.ppermute(x, axis, [(i, (i // 2 + step) % 4 * 2 + i % 2) for i in range(SIDE)])

def swap(x, axis):
    return lax.ppermute(x, axis, [(i, i ^ 1) for i in range(SIDE)])

def swap_group(x):
    return lax.ppermute(x, "grp", [(0, 1), (1, 0)])

ORDER = ((0, 0), (-1, 0), (1, 0), (2, 0), (0, 1), (-1, 1), (1, 1), (2, 1))

def near_col(x):
    return [x, shift(x, "col", 1), shift(x, "col", -1), shift(x, "col", 2), swap(x, "col")]

def rest_col(far, other):
    return [shift(other, "col", 1), shift(other, "col", -1), swap(far, "col")]

def gather_col(x):
    n = x.shape[0] // 2
    before, next_, other = shift(x, "col", 1), shift(x, "col", -1), swap(x, "col")
    far = jnp.concatenate([shift(before[:n], "col", 1), shift(next_[n:], "col", -1)], axis=0)
    return [x, before, next_, far, other, *rest_col(far, other)]

def fetch(refs, buffer, sems):
    copies = [pltpu.make_async_copy(ref, buffer.at[p], sems.at[p]) for p, ref in enumerate(refs)]
    for copy in copies:
        copy.start()
    return copies

def ids_of(axis):
    i = lax.axis_index(axis)
    return jnp.stack([(i // 2 + ring) % 4 * 2 + jnp.bitwise_xor(i % 2, pair) for ring, pair in ORDER]).astype(jnp.int32)

def place_of(block, axis):
    i = lax.axis_index(axis)
    ring = (block // 2 - i // 2) % 4
    first = jnp.where(ring == 3, 1, jnp.where(ring == 0, 0, ring + 1))
    return first + 4 * jnp.bitwise_xor(block % 2, i % 2)

def split(x):
    high = x.astype(bf16)
    return high, (x - high.astype(f32)).astype(bf16)

def dot3(a, b):
    left = jnp.concatenate([a[0], a[0], a[1]], axis=1)
    right = jnp.concatenate([b[0], b[1], b[0]], axis=0)
    return jnp.dot(left, right, preferred_element_type=f32)

def call(kernel, out, scalars, blocks, arrays, scratch, copies, work):
    return pl.pallas_call(
        kernel,
        out_shape=out,
        in_specs=[SMEM] * len(scalars) + [VMEM] * len(blocks) + [ANY] * len(arrays),
        out_specs=jax.tree.map(lambda _: VMEM, out),
        scratch_shapes=[pltpu.VMEM(s, d) for s, d in scratch] + [pltpu.SemaphoreType.DMA((copies,))],
        compiler_params=pltpu.CompilerParams(vmem_limit_bytes=60 * 2**20),
        cost_estimate=pl.CostEstimate(flops=work * 10**9, bytes_accessed=work * 3 * 10**6, transcendentals=0),
    )(*scalars, *blocks, *arrays)

def array(*shape, dtype=f32):
    return jax.ShapeDtypeStruct(shape, dtype)

def update_sum(cols, below, diag, below_buf, diag_buf, sems):
    n = len(below)
    below_in = fetch(below, below_buf, sems)
    diag_in = [
        pltpu.make_async_copy(
            diag.at[pl.ds(pl.multiple_of(cols[p] * WIDE, WIDE), WIDE)], diag_buf.at[p], sems.at[n + p]
        )
        for p in range(n)
    ]
    for copy in diag_in:
        copy.start()
    total = jnp.zeros((BAND, WIDE), f32)
    for p in range(n):
        below_in[p].wait()
        diag_in[p].wait()
        total += dot3(split(below_buf[p]), split(diag_buf[p]))
    return total

def update_near_kernel(cols, *rest):
    out, *scratch = rest[6:]
    out[...] = update_sum(cols, rest[:5], rest[5], *scratch)

def update_kernel(cols, row, live, part, *rest):
    flipped, *scratch = rest[4:]
    total = part[...] + update_sum(cols, rest[:3], rest[3], *scratch)
    ids = row[0] * BAND + lax.broadcasted_iota(jnp.int32, (BAND, WIDE), 0)
    flipped[...] = jnp.where(ids < live[0], total, 0.0).T

def pick_rows(place, source, out, first, count):
    step = 32

    def body(j, carry):
        at = pl.multiple_of(j * step, step)
        for i in range(0, step, 8):
            found = [source[pl.ds(place[first + at + i + k], 1), :] for k in range(8)]
            out[pl.ds(at + i, 8), :] = jnp.concatenate(found, axis=0)
        return carry

    lax.fori_loop(0, count // step, body, 0)

def root_rows_kernel(place, root, _, own, other, source, found, sems):
    copy = pltpu.make_async_copy(root, source, sems.at[0])
    copy.start()
    copy.wait()
    for half, out in enumerate((own, other)):
        pick_rows(place, source, found, half * BAND, BAND)
        out[...] = found[...].T

def coupling_kernel(place, row, live, *rest):
    update, pieces, out, update_buf, source, found, sems = rest[0], rest[1:9], *rest[9:]
    update_in = [
        pltpu.make_async_copy(update.at[pl.ds(p * WIDE, WIDE)], update_buf.at[p], sems.at[8 + p]) for p in range(8)
    ]
    pieces_in = [
        pltpu.make_async_copy(pieces[p], source.at[pl.ds(p * 2 * KEEP, 2 * KEEP)], sems.at[p]) for p in range(8)
    ]
    for copy in pieces_in + update_in:
        copy.start()
    for copy in pieces_in:
        copy.wait()
    total = jnp.zeros((WIDE, BAND), f32)
    for p in range(8):
        pick_rows(place, source, found, p * BAND, BAND)
        update_in[p].wait()
        total += dot3(split(update_buf[p]), split(found[...]))
    ids = row[0] * BAND + lax.broadcasted_iota(jnp.int32, (BAND, WIDE), 0)
    out[...] = jnp.where(ids < live[0], -total.T, 0.0)

def gram_kernel(diag, *rest):
    pieces, out, buffer, sems = rest[:8], *rest[9:]
    copies = fetch(pieces, buffer, sems)
    right = split(diag[...])
    for p in range(8):
        copies[p].wait()
        out[p] = dot3(split(buffer[p].T), right)

def partial_kernel(first, count, cols, coupling, *rest):
    update, gram, out, update_buf, gram_buf, out_buf, sems = rest[:count], rest[count], *rest[-5:]
    update_in = fetch(update, update_buf, sems)
    gram_in = [
        pltpu.make_async_copy(gram.at[first + p], gram_buf.at[p], sems.at[count + p]) for p in range(count)
    ]
    for copy in gram_in:
        copy.start()
    right = split(-coupling[...])
    sent = []
    for p in range(count):
        update_in[p].wait()
        gram_in[p].wait()
        out_buf[p] = gram_buf[p] + dot3(split(update_buf[p]), right)
        at = pl.ds(pl.multiple_of(cols[first + p] * WIDE, WIDE), WIDE)
        sent.append(pltpu.make_async_copy(out_buf.at[p], out.at[at], sems.at[2 * count + p]))
        sent[-1].start()
    for copy in sent:
        copy.wait()

def partial(first, update, cols, coupling, gram, onto=None):
    count = len(update)
    given = [cols, coupling, *update, gram] + ([] if onto is None else [onto])
    return pl.pallas_call(
        functools.partial(partial_kernel, first, count),
        out_shape=array(SEP, WIDE),
        in_specs=[SMEM, VMEM] + [ANY] * (len(given) - 2),
        out_specs=ANY,
        scratch_shapes=[
            pltpu.VMEM((count, WIDE, BAND), f32),
            pltpu.VMEM((count, WIDE, WIDE), f32),
            pltpu.VMEM((count, WIDE, WIDE), f32),
            pltpu.SemaphoreType.DMA((3 * count,)),
        ],
        input_output_aliases={} if onto is None else {len(given) - 1: 0},
        compiler_params=pltpu.CompilerParams(vmem_limit_bytes=60 * 2**20),
        cost_estimate=pl.CostEstimate(flops=count * 10**9, bytes_accessed=count * 3 * 10**6, transcendentals=0),
    )(*given)

def per_device(root_inverse, ancestor_map, live_rows, factor_below, diag_inverse, tile_mask):
    row, group = lax.axis_index("row"), lax.axis_index("grp")
    cols = ids_of("col")
    diag_block = diag_inverse[0]
    own_map = ancestor_map[0]
    other_map = swap_group(own_map)

    root_cols = lax.all_gather(root_inverse, "row", axis=0, tiled=True)

    diag_cols = lax.all_gather(diag_block, "row", axis=0, tiled=True)

    diag_all = gather_col(diag_block)
    tile_keep = jnp.repeat(jnp.repeat(tile_mask[0], TILE, axis=0), TILE, axis=1).astype(f32)
    below, other_map = hold([factor_below[0] * tile_keep, other_map[None]], diag_all)

    gram = call(
        gram_kernel, array(SIDE, WIDE, WIDE), [], [diag_block], diag_all + [below], [((SIDE, WIDE, WIDE), f32)], 8, 12
    )
    place = jnp.concatenate([lax.dynamic_slice_in_dim(m, row * BAND, BAND) for m in (own_map, other_map[0])])
    own_rows, other_rows = call(
        root_rows_kernel, (array(KEEP, BAND), array(KEEP, BAND)), [place], [], [root_cols, below],
        [((ROOT, KEEP), f32), ((BAND, KEEP), f32)], 1, 5,
    )
    below_near = near_col(below)
    *below_near, gram, other_rows = hold([*below_near, gram, swap_group(other_rows)], [])
    below_rest = rest_col(*below_near[3:])
    part = call(
        update_near_kernel, array(BAND, WIDE), [cols[:5]], [], below_near + [diag_cols],
        [((5, BAND, WIDE), f32), ((5, WIDE, WIDE), f32)], 10, 5,
    )
    picked = jnp.concatenate([own_rows, other_rows], axis=0)
    picked, part = hold([picked, part], below_rest)

    flipped = call(
        update_kernel, array(WIDE, BAND), [cols[5:], row[None], live_rows], [part], below_rest + [diag_cols],
        [((3, BAND, WIDE), f32), ((3, WIDE, WIDE), f32)], 6, 3,
    )
    update_rows = lax.all_gather(flipped, "row", axis=0, tiled=True)
    picked_all = gather_col(picked)
    flipped, gram = hold([flipped, gram], picked_all)

    half = (own_map // (ROOT // 2) != group).astype(jnp.int32)
    place = place_of(own_map % (ROOT // 2) // KEEP, "col") * (2 * KEEP) + half * KEEP + own_map % KEEP
    coupling = call(
        coupling_kernel, array(BAND, WIDE), [place, row[None], live_rows], [], [update_rows] + picked_all,
        [((SIDE, WIDE, BAND), f32), ((ROOT, BAND), f32), ((BAND, BAND), f32)], 16, 12,
    )
    update_near = near_col(flipped)

    update_rest = rest_col(*update_near[3:])
    total = partial(0, update_near, cols, coupling, gram)
    (total,) = hold([total], update_rest)
    total = partial(5, update_rest, cols, coupling, gram, total)
    separator = lax.psum_scatter(total, "row", scatter_dimension=0, tiled=True)
    return (coupling[None], separator[None])

def solution(mesh):
    return jax.shard_map(
        per_device,
        mesh=mesh,
        in_specs=(
            P("row", ("grp", "col")),
            P("grp", None),
            P("grp"),
            P("grp", "row", "col"),
            P("grp", "row", "col"),
            P("grp", "row", "col"),
        ),
        out_specs=(P("grp", "row", "col"), P("grp", "row", "col")),
        check_vma=False,
    )
```

```python
import functools

import jax
import jax.numpy as jnp
from jax import lax
from jax.experimental import pallas as pl
from jax.experimental.pallas import tpu as pltpu
from jax.sharding import PartitionSpec as P

ROOT = 4096
SEP = 3072
ANC = 2048
TILE = 128
SIDE = 8
BAND = ANC // SIDE
WIDE = SEP // SIDE
KEEP = ROOT // (2 * SIDE)

f32 = jnp.float32
bf16 = jnp.bfloat16
VMEM = pl.BlockSpec(memory_space=pltpu.VMEM)
SMEM = pl.BlockSpec(memory_space=pltpu.SMEM)
ANY = pl.BlockSpec(memory_space=pl.ANY)

def hold(arrays, deps):
    n = len(arrays)
    return pl.pallas_call(
        lambda *refs: None,
        out_shape=[jax.ShapeDtypeStruct(x.shape, x.dtype) for x in arrays],
        in_specs=[ANY] * (n + len(deps)),
        out_specs=[ANY] * n,
        input_output_aliases={i: i for i in range(n)},
        compiler_params=pltpu.CompilerParams(vmem_limit_bytes=60 * 2**20),
    )(*arrays, *deps)

def shift(x, axis, step):
    return lax.ppermute(x, axis, [(i, (i // 2 + step) % 4 * 2 + i % 2) for i in range(SIDE)])

def swap(x, axis):
    return lax.ppermute(x, axis, [(i, i ^ 1) for i in range(SIDE)])

def swap_group(x):
    return lax.ppermute(x, "grp", [(0, 1), (1, 0)])

ORDER = ((0, 0), (-1, 0), (1, 0), (2, 0), (0, 1), (-1, 1), (1, 1), (2, 1))

def near_col(x):
    return [x, shift(x, "col", 1), shift(x, "col", -1), shift(x, "col", 2), swap(x, "col")]

def rest_col(far, other):
    return [shift(other, "col", 1), shift(other, "col", -1), swap(far, "col")]

def gather_col(x):
    n = x.shape[0] // 2
    before, next_, other = shift(x, "col", 1), shift(x, "col", -1), swap(x, "col")
    far = jnp.concatenate([shift(before[:n], "col", 1), shift(next_[n:], "col", -1)], axis=0)
    return [x, before, next_, far, other, *rest_col(far, other)]

def fetch(refs, buffer, sems):
    copies = [pltpu.make_async_copy(ref, buffer.at[p], sems.at[p]) for p, ref in enumerate(refs)]
    for copy in copies:
        copy.start()
    return copies

def ids_of(axis):
    i = lax.axis_index(axis)
    return jnp.stack([(i // 2 + ring) % 4 * 2 + jnp.bitwise_xor(i % 2, pair) for ring, pair in ORDER]).astype(jnp.int32)

def place_of(block, axis):
    i = lax.axis_index(axis)
    ring = (block // 2 - i // 2) % 4
    first = jnp.where(ring == 3, 1, jnp.where(ring == 0, 0, ring + 1))
    return first + 4 * jnp.bitwise_xor(block % 2, i % 2)

def split(x):
    high = x.astype(bf16)
    return high, (x - high.astype(f32)).astype(bf16)

def dot3(a, b):
    left = jnp.concatenate([a[0], a[0], a[1]], axis=1)
    right = jnp.concatenate([b[0], b[1], b[0]], axis=0)
    return jnp.dot(left, right, preferred_element_type=f32)

def call(kernel, out, scalars, blocks, arrays, scratch, copies, work):
    return pl.pallas_call(
        kernel,
        out_shape=out,
        in_specs=[SMEM] * len(scalars) + [VMEM] * len(blocks) + [ANY] * len(arrays),
        out_specs=jax.tree.map(lambda _: VMEM, out),
        scratch_shapes=[pltpu.VMEM(s, d) for s, d in scratch] + [pltpu.SemaphoreType.DMA((copies,))],
        compiler_params=pltpu.CompilerParams(vmem_limit_bytes=60 * 2**20),
        cost_estimate=pl.CostEstimate(flops=work * 10**9, bytes_accessed=work * 3 * 10**6, transcendentals=0),
    )(*scalars, *blocks, *arrays)

def array(*shape, dtype=f32):
    return jax.ShapeDtypeStruct(shape, dtype)

def update_sum(cols, below, diag, below_buf, diag_buf, sems):
    n = len(below)
    below_in = fetch(below, below_buf, sems)
    diag_in = [
        pltpu.make_async_copy(
            diag.at[pl.ds(pl.multiple_of(cols[p] * WIDE, WIDE), WIDE)], diag_buf.at[p], sems.at[n + p]
        )
        for p in range(n)
    ]
    for copy in diag_in:
        copy.start()
    total = jnp.zeros((BAND, WIDE), f32)
    for p in range(n):
        below_in[p].wait()
        diag_in[p].wait()
        total += dot3(split(below_buf[p]), split(diag_buf[p]))
    return total

def update_near_kernel(cols, *rest):
    out, *scratch = rest[6:]
    out[...] = update_sum(cols, rest[:5], rest[5], *scratch)

def update_kernel(cols, row, live, part, *rest):
    flipped, *scratch = rest[4:]
    total = part[...] + update_sum(cols, rest[:3], rest[3], *scratch)
    ids = row[0] * BAND + lax.broadcasted_iota(jnp.int32, (BAND, WIDE), 0)
    flipped[...] = jnp.where(ids < live[0], total, 0.0).T

def pick_rows(place, source, out, first, count):
    step = 32

    def body(j, carry):
        at = pl.multiple_of(j * step, step)
        for i in range(0, step, 8):
            found = [source[pl.ds(place[first + at + i + k], 1), :] for k in range(8)]
            out[pl.ds(at + i, 8), :] = jnp.concatenate(found, axis=0)
        return carry

    lax.fori_loop(0, count // step, body, 0)

def root_rows_kernel(place, root, _, own, other, source, found, sems):
    copy = pltpu.make_async_copy(root, source, sems.at[0])
    copy.start()
    copy.wait()
    for half, out in enumerate((own, other)):
        pick_rows(place, source, found, half * BAND, BAND)
        out[...] = found[...].T

def coupling_kernel(place, row, live, *rest):
    update, pieces, out, update_buf, source, found, sems = rest[0], rest[1:9], *rest[9:]
    update_in = [
        pltpu.make_async_copy(update.at[pl.ds(p * WIDE, WIDE)], update_buf.at[p], sems.at[8 + p]) for p in range(8)
    ]
    pieces_in = [
        pltpu.make_async_copy(pieces[p], source.at[pl.ds(p * 2 * KEEP, 2 * KEEP)], sems.at[p]) for p in range(8)
    ]
    for copy in pieces_in + update_in:
        copy.start()
    for copy in pieces_in:
        copy.wait()
    total = jnp.zeros((WIDE, BAND), f32)
    for p in range(8):
        pick_rows(place, source, found, p * BAND, BAND)
        update_in[p].wait()
        total += dot3(split(update_buf[p]), split(found[...]))
    ids = row[0] * BAND + lax.broadcasted_iota(jnp.int32, (BAND, WIDE), 0)
    out[...] = jnp.where(ids < live[0], -total.T, 0.0)

def gram_kernel(diag, *rest):
    pieces, out, buffer, sems = rest[:8], *rest[9:]
    copies = fetch(pieces, buffer, sems)
    right = split(diag[...])
    for p in range(8):
        copies[p].wait()
        out[p] = dot3(split(buffer[p].T), right)

def partial_kernel(first, count, cols, coupling, *rest):
    update, gram, out, update_buf, gram_buf, out_buf, sems = rest[:count], rest[count], *rest[-5:]
    update_in = fetch(update, update_buf, sems)
    gram_in = [
        pltpu.make_async_copy(gram.at[first + p], gram_buf.at[p], sems.at[count + p]) for p in range(count)
    ]
    for copy in gram_in:
        copy.start()
    right = split(-coupling[...])
    sent = []
    for p in range(count):
        update_in[p].wait()
        gram_in[p].wait()
        out_buf[p] = gram_buf[p] + dot3(split(update_buf[p]), right)
        at = pl.ds(pl.multiple_of(cols[first + p] * WIDE, WIDE), WIDE)
        sent.append(pltpu.make_async_copy(out_buf.at[p], out.at[at], sems.at[2 * count + p]))
        sent[-1].start()
    for copy in sent:
        copy.wait()

def partial(first, update, cols, coupling, gram, onto=None):
    count = len(update)
    given = [cols, coupling, *update, gram] + ([] if onto is None else [onto])
    return pl.pallas_call(
        functools.partial(partial_kernel, first, count),
        out_shape=array(SEP, WIDE),
        in_specs=[SMEM, VMEM] + [ANY] * (len(given) - 2),
        out_specs=ANY,
        scratch_shapes=[
            pltpu.VMEM((count, WIDE, BAND), f32),
            pltpu.VMEM((count, WIDE, WIDE), f32),
            pltpu.VMEM((count, WIDE, WIDE), f32),
            pltpu.SemaphoreType.DMA((3 * count,)),
        ],
        input_output_aliases={} if onto is None else {len(given) - 1: 0},
        compiler_params=pltpu.CompilerParams(vmem_limit_bytes=60 * 2**20),
        cost_estimate=pl.CostEstimate(flops=count * 10**9, bytes_accessed=count * 3 * 10**6, transcendentals=0),
    )(*given)

def per_device(root_inverse, ancestor_map, live_rows, factor_below, diag_inverse, tile_mask):
    row, group = lax.axis_index("row"), lax.axis_index("grp")
    cols = ids_of("col")
    diag_block = diag_inverse[0]
    own_map = ancestor_map[0]
    other_map = swap_group(own_map)

    root_cols = lax.all_gather(root_inverse, "row", axis=0, tiled=True)

    diag_cols = lax.all_gather(diag_block, "row", axis=0, tiled=True)

    diag_all = gather_col(diag_block)
    tile_keep = jnp.repeat(jnp.repeat(tile_mask[0], TILE, axis=0), TILE, axis=1).astype(f32)
    below, other_map = hold([factor_below[0] * tile_keep, other_map[None]], diag_all)

    gram = call(
        gram_kernel, array(SIDE, WIDE, WIDE), [], [diag_block], diag_all + [below], [((SIDE, WIDE, WIDE), f32)], 8, 12
    )
    place = jnp.concatenate([lax.dynamic_slice_in_dim(m, row * BAND, BAND) for m in (own_map, other_map[0])])
    own_rows, other_rows = call(
        root_rows_kernel, (array(KEEP, BAND), array(KEEP, BAND)), [place], [], [root_cols, below],
        [((ROOT, KEEP), f32), ((BAND, KEEP), f32)], 1, 5,
    )
    below_near = near_col(below)
    *below_near, gram, other_rows = hold([*below_near, gram, swap_group(other_rows)], [])
    below_rest = rest_col(*below_near[3:])
    part = call(
        update_near_kernel, array(BAND, WIDE), [cols[:5]], [], below_near + [diag_cols],
        [((5, BAND, WIDE), f32), ((5, WIDE, WIDE), f32)], 10, 5,
    )
    picked = jnp.concatenate([own_rows, other_rows], axis=0)
    picked, part = hold([picked, part], below_rest)

    flipped = call(
        update_kernel, array(WIDE, BAND), [cols[5:], row[None], live_rows], [part], below_rest + [diag_cols],
        [((3, BAND, WIDE), f32), ((3, WIDE, WIDE), f32)], 6, 3,
    )
    update_rows = lax.all_gather(flipped, "row", axis=0, tiled=True)
    picked_all = gather_col(picked)
    flipped, gram = hold([flipped, gram], picked_all)

    half = (own_map // (ROOT // 2) != group).astype(jnp.int32)
    place = place_of(own_map % (ROOT // 2) // KEEP, "col") * (2 * KEEP) + half * KEEP + own_map % KEEP
    coupling = call(
        coupling_kernel, array(BAND, WIDE), [place, row[None], live_rows], [], [update_rows] + picked_all,
        [((SIDE, WIDE, BAND), f32), ((ROOT, BAND), f32), ((BAND, BAND), f32)], 16, 12,
    )
    update_all = gather_col(flipped)
    update_near, update_rest = update_all[:5], update_all[5:]
    total = partial(0, update_near, cols, coupling, gram)
    (total,) = hold([total], update_rest)
    total = partial(5, update_rest, cols, coupling, gram, total)
    separator = lax.psum_scatter(total, "row", scatter_dimension=0, tiled=True)
    return (coupling[None], separator[None])

def solution(mesh):
    return jax.shard_map(
        per_device,
        mesh=mesh,
        in_specs=(
            P("row", ("grp", "col")),
            P("grp", None),
            P("grp"),
            P("grp", "row", "col"),
            P("grp", "row", "col"),
            P("grp", "row", "col"),
        ),
        out_specs=(P("grp", "row", "col"), P("grp", "row", "col")),
        check_vma=False,
    )
```
